32 devices in a mesh: groups: 2 (over x), srv: 16 (over z, y, core).
Axes of the slice: x: 2, y: 2, z: 4, core: 2. Of those that a mesh axis runs over, the one named last changes fastest.
Arguments:
- fields: bfloat16 [384, 336, 128], P(('groups', 'srv')), parts along dimension 0, may hold values from -6 to 6
- tile_count: int32 [192], P('srv'), may hold values from 32 to 128
- route: int32 [16, 16, 2], P('srv'), may hold values from 0 to 11, as said below
- weights: bfloat16 [9216, 128, 128], P('srv'), may hold values from -0.1875 to 0.1875
- block_src: int32 [9216], P('srv'), may hold values from 0 to 31, as said below
- destination_block: int32 [9216], P('srv'), may hold values from 0 to 255, as said below
- block_live: int32 [9216], P('srv'), may hold values from 0 to 1, as said below
Outputs:
- remapped: bfloat16 [512, 336, 128], P(('groups', 'srv')), parts along dimension 0
The draws below stay inside these ranges and needn't reach their ends.
There are 2 independent parts, one for each index of `groups`. The reference program is written for one: setup_inputs(seed, part) draws one part's arguments, and reference() takes and returns one part's arrays. A program takes and returns all parts, laid end to end along the dimension named above; an argument that names none is the same for every part. Nothing has to cross between parts.
Inputs may be any that keep to these rules, and one draw needn't show every extreme that they name: route[s, d] lists 2 different blocks of compute rank d, as indices among its 12 blocks; every server needs exactly 2 blocks of every rank. block_src[k] = d * 2 + j names entry j of route[s, d] for the slot's server s = k // 576. `destination_block`: a slot of server s adds to one of the destination blocks (s * 16 + i) % 256 with 0 <= i <= 16: its own band or the first block of the next server's band. `block_live`: the live slots of each server come first among its 576 slots; some server has all of them live.
All inputs are finite; a program needn't handle non-finite values.
Results may differ from the reference program's by a relative error of at most 0.001.
Values may be sent and summed in bfloat16 or wider, within the bound.
A program may use at most 128 MiB of HBM per device.

```python
import jax
import jax.numpy as jnp
from jax import lax

BLOCK_CELLS = 128
CAP = 2
SB_DEV = 12
DB_DEV = 16
NNZ_DEV = 576
ROWS = 336
SBLK = 192
DBLK = 256
TOTAL_SLOTS = 9216
N_SRV = 16


def draw_route(key, part):
    servers = SBLK // SB_DEV
    scores = jax.random.randint(jax.random.fold_in(key, 3), (servers, servers, SB_DEV), 0, 1 << 20)
    scores = scores * SB_DEV + jnp.arange(SB_DEV, dtype=jnp.int32)
    ranked = jnp.argsort(scores, axis=-1, stable=True)
    return ranked[:, :, :CAP].astype(jnp.int32)


def block_pattern(key):
    servers = SBLK // SB_DEV
    requested = servers * CAP
    keys = jax.random.split(jax.random.fold_in(key, 7), 4)
    slot_ids = jnp.arange(NNZ_DEV, dtype=jnp.int32)[None, :]
    sources = jax.random.randint(keys[0], (servers, NNZ_DEV), 0, requested)
    sources = jnp.where(slot_ids < requested, slot_ids, sources)
    local_rows = jax.random.randint(keys[1], (servers, NNZ_DEV), 0, DB_DEV + 1)
    local_rows = jnp.where(slot_ids < DB_DEV + 1, slot_ids, local_rows)
    live_count = jax.random.randint(keys[2], (servers,), NNZ_DEV // 6, NNZ_DEV // 2 + 1)
    shuffled = jax.random.permutation(keys[3], servers)
    live_count = jnp.where(shuffled < max(1, servers // 8), NNZ_DEV, live_count)
    living = (slot_ids < live_count[:, None]).astype(jnp.int32)
    owners = jnp.arange(servers, dtype=jnp.int32)[:, None]
    targets = jnp.mod(owners * DB_DEV + local_rows, servers * DB_DEV)
    return (sources.reshape(-1).astype(jnp.int32), targets.reshape(-1).astype(jnp.int32), living.reshape(-1))


def draw_block_src(key, part):
    return block_pattern(key)[0]


def draw_destination_block(key, part):
    return block_pattern(key)[1]


def draw_block_live(key, part):
    return block_pattern(key)[2]


def plant(result, key, smallest, largest):
    longest = result.shape.index(max(result.shape))
    spots = []
    for shift in (0, 1):
        where = [jax.random.randint(jax.random.fold_in(key, axis), (), 0, length) for axis, length in enumerate(result.shape)]
        where[longest] = (where[longest] + shift) % result.shape[longest]
        spots.append(tuple(where))
    return result.at[spots[0]].set(smallest).at[spots[1]].set(largest)


def shard_levels(rng, shape, shards, least, high):
    gain, own = 1.0, jax.random.fold_in(rng, 6)
    for position, parts in shards:
        draws = jnp.exp(jax.random.uniform(jax.random.fold_in(own, position), (parts,), jnp.float32, least / len(shards), high / len(shards)))
        gain = gain * jnp.repeat(draws, shape[position] // parts).reshape([-1 if axis == position else 1 for axis in range(len(shape))])
    return gain


def centred(rng, extent, scale, limit, cuts=(), held_as=jnp.bfloat16):
    factor_of = shard_levels(rng, extent, cuts, -0.22, 0.18) if cuts else 1.0
    entries = jax.random.normal(rng, extent, jnp.float32) * scale * factor_of
    return jnp.minimum(jnp.maximum(entries, -limit), limit).astype(held_as)


def setup_inputs(seed: int = 0, part: int = 0) -> dict:
    arg_keys = jax.random.split(jax.random.key(seed), 8)
    part_splits = jax.random.split(jax.random.fold_in(arg_keys[7], part), 8)
    fields = centred(part_splits[0], (SBLK, ROWS, BLOCK_CELLS), 1.0, 6.0, ((0, 16),))
    tile_count = plant(jax.random.randint(arg_keys[1], (SBLK,), BLOCK_CELLS // 4, BLOCK_CELLS + 1), jax.random.fold_in(arg_keys[1], 1), BLOCK_CELLS // 4, BLOCK_CELLS).astype(jnp.int32)
    route = draw_route(jax.random.fold_in(arg_keys[7], 71), part)
    weights = centred(arg_keys[3], (TOTAL_SLOTS, BLOCK_CELLS, BLOCK_CELLS), (BLOCK_CELLS * 8) ** -0.5, 0.1875, ((0, 16),))
    block_src = draw_block_src(jax.random.fold_in(arg_keys[7], 71), part)
    destination_block = draw_destination_block(jax.random.fold_in(arg_keys[7], 71), part)
    block_live = draw_block_live(jax.random.fold_in(arg_keys[7], 71), part)
    return {"fields": fields, "tile_count": tile_count, "route": route, "weights": weights, "block_src": block_src, "destination_block": destination_block, "block_live": block_live}


slot_group = 32


def reference(fields, tile_count, route, weights, block_src, destination_block, block_live):
    positions = jnp.arange(BLOCK_CELLS, dtype=jnp.int32)
    keeper = positions[None, None, :] < tile_count[:, None, None]
    masked = jnp.where(keeper, fields, jnp.zeros_like(fields))
    owners = jnp.arange(N_SRV, dtype=jnp.int32)
    targets = jnp.arange(DB_DEV + 1, dtype=jnp.int32)
    groups = NNZ_DEV // slot_group

    def serve(server):
        wanted = (owners[:, None] * SB_DEV + route[server]).reshape(-1).astype(jnp.int32)
        received = masked[wanted].astype(jnp.float32)
        first_slot = (server * NNZ_DEV).astype(jnp.int32)
        w_local = lax.dynamic_slice_in_dim(weights, first_slot, NNZ_DEV, 0)
        source_local = lax.dynamic_slice_in_dim(block_src, first_slot, NNZ_DEV, 0)
        dst_local = lax.dynamic_slice_in_dim(destination_block, first_slot, NNZ_DEV, 0)
        live_local = lax.dynamic_slice_in_dim(block_live, first_slot, NNZ_DEV, 0)
        local_rows = jnp.mod(dst_local - server * DB_DEV, DBLK)
        selector = ((local_rows[:, None] == targets[None, :]) & (live_local[:, None] == 1)).astype(jnp.float32)

        def accumulate(totals, piece_set):
            w_group, source_group, select_group = piece_set
            weighted_products = jnp.einsum("krc,kdc->krd", received[source_group], w_group.astype(jnp.float32),
                                  precision=lax.Precision.HIGHEST)
            return totals + jnp.einsum("kj,krd->jrd", select_group, weighted_products,
                                       precision=lax.Precision.HIGHEST), None

        start_totals = jnp.zeros((DB_DEV + 1, ROWS, BLOCK_CELLS), jnp.float32)
        totals, _ = lax.scan(accumulate, start_totals,
                             (w_local.reshape(groups, slot_group, BLOCK_CELLS, BLOCK_CELLS),
                              source_local.reshape(groups, slot_group),
                              selector.reshape(groups, slot_group, DB_DEV + 1)))
        return totals

    partial_sums = lax.map(serve, owners)
    owned_rows = partial_sums[:, :DB_DEV]
    excess_count = jnp.roll(partial_sums[:, DB_DEV], 1, axis=0)
    owned_rows = owned_rows.at[:, 0].add(excess_count)
    return owned_rows.reshape(DBLK, ROWS, BLOCK_CELLS).astype(jnp.bfloat16)
```

```python
import functools

import jax
import jax.numpy as jnp
from jax import lax
from jax.experimental import pallas as pl
from jax.experimental.pallas import tpu as pltpu
from jax.sharding import PartitionSpec as P

DB_DEV = 16
UNIT = 4
RING = 24


def plan(bucket, valid, n_buckets, source, steps_max):
    slots = bucket.shape[0]
    zero_source = -1
    ids = jnp.arange(n_buckets, dtype=jnp.int32)
    member = (bucket[None, :] == ids[:, None]) & valid[None, :]
    steps = (jnp.sum(member.astype(jnp.int32), axis=1) + UNIT - 1) // UNIT
    edges = jnp.arange(n_buckets + 1, dtype=jnp.int32)
    starts = jnp.sum(jnp.where(ids[None, :] < edges[:, None], steps[None, :], 0), axis=1)
    index = jnp.arange(slots, dtype=jnp.int32)
    before = jnp.sum(
        ((bucket[None, :] == bucket[:, None]) & valid[None, :] & (index[None, :] < index[:, None])).astype(jnp.int32),
        axis=1,
    )
    own = jnp.sum(jnp.where(ids[None, :] < bucket[:, None], steps[None, :], 0), axis=1)
    place = jnp.where(valid, own * UNIT + before, -1)
    places = jnp.arange(steps_max * UNIT, dtype=jnp.int32)
    hit = places[:, None] == place[None, :]
    slot = jnp.sum(jnp.where(hit, index[None, :], 0), axis=1)
    src = jnp.sum(jnp.where(hit, source[None, :] - zero_source, 0), axis=1) + zero_source
    return starts, slot, src


def product_kernel(first, last, finish, starts, slot, src, x_hbm, w_hbm, *refs):
    if finish is None:
        out, x, ring, x_sem, w_sem = refs
        prev = None
    else:
        prev, *refs = refs
        *outs, x, ring, acc, x_sem, w_sem = refs
    blocks = x_hbm.shape[0]
    load = pltpu.make_async_copy(x_hbm, x.at[pl.ds(0, blocks)], x_sem)
    load.start()
    begin, end = starts[first], starts[last]

    def fetch(p):
        for u in range(UNIT):
            pltpu.make_async_copy(
                w_hbm.at[slot[p * UNIT + u]], ring.at[lax.rem(p, RING), u], w_sem.at[lax.rem(p, RING)]
            ).start()

    def prime(p, carry):
        fetch(p)
        return carry

    lax.fori_loop(begin, jnp.minimum(end, begin + RING), prime, 0)
    x[blocks] = jnp.zeros(x.shape[1:], x.dtype)
    load.wait()

    def step(total, p, carry):
        at = lax.rem(p, RING)
        pltpu.make_async_copy(ring.at[at], ring.at[at], w_sem.at[at]).wait()
        lhs = jnp.concatenate([x[jnp.where(src[p * UNIT + u] < 0, blocks, src[p * UNIT + u])] for u in range(UNIT)], axis=1)
        rhs = jnp.concatenate([ring[at, u] for u in range(UNIT)], axis=1)
        total[...] += lax.dot_general(lhs, rhs, (((1,), (1,)), ((), ())), preferred_element_type=jnp.float32)

        @pl.when(p + RING < end)
        def _():
            fetch(p + RING)

        return carry

    def bucket(b, carry):
        if finish is None:
            total = out.at[b - first]
            total[...] = jnp.zeros(total.shape, total.dtype)
        else:
            total = acc
            total[...] = prev[b - first]
        lax.fori_loop(starts[b], starts[b + 1], functools.partial(step, total), 0)
        if finish is not None:
            finish(b - first, total, outs)
        return carry

    lax.fori_loop(first, last, bucket, 0)


def products(starts, slot, src, x, w, first, last, prev=None, finish=None, out_shape=None):
    blocks, rows, width = x.shape
    if finish is None:
        out_shape = jax.ShapeDtypeStruct((last - first, rows, width), jnp.float32)
        acc = []
    else:
        acc = [pltpu.VMEM((rows, width), jnp.float32)]
    smem = pl.BlockSpec(memory_space=pltpu.SMEM)
    hbm = pl.BlockSpec(memory_space=pl.ANY)
    vmem = pl.BlockSpec(memory_space=pltpu.VMEM)
    ins = [starts, slot, src, x, w] + ([] if prev is None else [prev])
    n_slots = w.shape[0] * (last - first) // 34
    return pl.pallas_call(
        functools.partial(product_kernel, first, last, finish),
        out_shape=out_shape,
        in_specs=[smem] * 3 + [hbm] * 2 + ([] if prev is None else [vmem]),
        out_specs=jax.tree.map(lambda _: vmem, out_shape),
        scratch_shapes=[
            pltpu.VMEM((blocks + 1, rows, width), x.dtype),
            pltpu.VMEM((RING, UNIT, width, width), w.dtype),
            *acc,
            pltpu.SemaphoreType.DMA,
            pltpu.SemaphoreType.DMA((RING,)),
        ],
        compiler_params=pltpu.CompilerParams(vmem_limit_bytes=24 << 20),
        cost_estimate=pl.CostEstimate(
            flops=4 * n_slots * rows * width * width, bytes_accessed=4 * n_slots * width * width, transcendentals=0
        ),
    )(*ins)


def select_kernel(demanded, tile_count, fields, *outs):
    servers = outs[0].shape[0]
    rows, width = fields.shape[1:]
    cells = lax.broadcasted_iota(jnp.int32, (rows, width), 1)

    def serve(s, carry):
        for j, out in enumerate(outs):
            block = demanded[s * len(outs) + j]
            kept = jnp.where(cells < tile_count[block], fields[block].astype(jnp.float32), 0.0)
            out[s] = kept.astype(fields.dtype)
        return carry

    lax.fori_loop(0, servers, serve, 0)


def select(demanded, tile_count, fields):
    servers, capacity = demanded.shape
    smem = pl.BlockSpec(memory_space=pltpu.SMEM)
    vmem = pl.BlockSpec(memory_space=pltpu.VMEM)
    return pl.pallas_call(
        select_kernel,
        out_shape=[jax.ShapeDtypeStruct((servers, *fields.shape[1:]), fields.dtype)] * capacity,
        in_specs=[smem, smem, vmem],
        out_specs=[vmem] * capacity,
        compiler_params=pltpu.CompilerParams(vmem_limit_bytes=24 << 20),
    )(demanded.reshape(-1), tile_count, fields)


def finish_rows(i, total, outs):
    out, head = outs

    @pl.when(i == 0)
    def _():
        head[...] = total[...]

    out[i] = total[...].astype(out.dtype)


def finish_excess(i, total, outs):
    outs[0][...] = total[...]


def shards(fields, tile_count, route, weights, block_src, destination_block, block_live):
    servers = lax.axis_size("srv")
    server = lax.axis_index("srv")
    held, rows, width = fields.shape
    slots = weights.shape[0]
    capacity = route.shape[2]
    band = DB_DEV
    demanded = lax.all_to_all(route[0], "srv", split_axis=0, concat_axis=0, tiled=True)
    received = [
        lax.all_to_all(part, "srv", split_axis=0, concat_axis=0, tiled=True)
        for part in select(demanded, tile_count, fields)
    ]
    local = jnp.mod(destination_block - server * band, band * servers)
    entry, rank = block_src % capacity, block_src // capacity
    n_rows = band + 1
    steps_max = -(-slots // UNIT) + capacity * n_rows
    starts, slot, src = plan(entry * n_rows + local, block_live == 1, capacity * n_rows, rank, steps_max)
    totals = products(starts, slot, src, received[0], weights, 0, n_rows)
    piece = jax.ShapeDtypeStruct((rows, width), jnp.float32)
    (excess,) = products(
        starts, slot, src, received[1], weights, n_rows + band, n_rows + n_rows, totals[band:], finish_excess, (piece,)
    )
    arrived = lax.ppermute(excess, "srv", [(i, (i + 1) % servers) for i in range(servers)])
    body = jax.ShapeDtypeStruct((band, rows, width), jnp.bfloat16)
    out, head = products(
        starts, slot, src, received[1], weights, n_rows, n_rows + band, totals[:band], finish_rows, (body, piece)
    )
    return out.at[0].set((head + arrived).astype(jnp.bfloat16))


def solution(mesh):
    in_specs = (
        P(("groups", "srv"), None, None),
        P("srv"),
        P("srv", None, None),
        P("srv", None, None),
        P("srv"),
        P("srv"),
        P("srv"),
    )
    out_specs = P(("groups", "srv"), None, None)
    return jax.shard_map(shards, mesh=mesh, in_specs=in_specs, out_specs=out_specs, check_vma=False)
```

```python
import functools

import jax
import jax.numpy as jnp
from jax import lax
from jax.experimental import pallas as pl
from jax.experimental.pallas import tpu as pltpu
from jax.sharding import PartitionSpec as P

DB_DEV = 16
UNIT = 4
RING = 24
LIMIT = 54 << 20


def plan(bucket, valid, n_buckets, source, steps_max):
    slots = bucket.shape[0]
    zero_source = -1
    ids = jnp.arange(n_buckets, dtype=jnp.int32)
    member = (bucket[None, :] == ids[:, None]) & valid[None, :]
    steps = (jnp.sum(member.astype(jnp.int32), axis=1) + UNIT - 1) // UNIT
    edges = jnp.arange(n_buckets + 1, dtype=jnp.int32)
    starts = jnp.sum(jnp.where(ids[None, :] < edges[:, None], steps[None, :], 0), axis=1)
    index = jnp.arange(slots, dtype=jnp.int32)
    before = jnp.sum(
        ((bucket[None, :] == bucket[:, None]) & valid[None, :] & (index[None, :] < index[:, None])).astype(jnp.int32),
        axis=1,
    )
    own = jnp.sum(jnp.where(ids[None, :] < bucket[:, None], steps[None, :], 0), axis=1)
    place = jnp.where(valid, own * UNIT + before, -1)
    places = jnp.arange(steps_max * UNIT, dtype=jnp.int32)
    hit = places[:, None] == place[None, :]
    slot = jnp.sum(jnp.where(hit, index[None, :], 0), axis=1)
    src = jnp.sum(jnp.where(hit, source[None, :] - zero_source, 0), axis=1) + zero_source
    return starts, slot, src


def contract(blocks, factors):
    return lax.dot_general(
        jnp.concatenate(blocks, axis=1),
        jnp.concatenate(factors, axis=1),
        (((1,), (1,)), ((), ())),
        preferred_element_type=jnp.float32,
    )


def exchange_kernel(
    n, steps, tile_count, near_slot, near_src, keep, last, used,
    wanted, fields, w_hbm,
    near, far, totals,
    asked, asked_now, outgoing, held, prefix,
    ask_send, ask_recv, send_sem, recv_sem, own_sem, w_sem,
):
    me = lax.axis_index("srv")
    half = n // 2
    rows, width = fields.shape[1:]
    capacity = outgoing.shape[1]
    blocks = half * capacity
    load = pltpu.make_async_copy(w_hbm, held, w_sem)
    load.start()

    def partner(i):
        return lax.rem(me + half + ((i + 1) // 2) * (2 * ((i + 1) % 2) - 1), n)

    barrier = pltpu.get_barrier_semaphore()

    def greet(i, carry):
        pl.semaphore_signal(barrier, inc=1, device_id={"srv": partner(i)}, device_id_type=pl.DeviceIdType.MESH)
        return carry

    lax.fori_loop(0, n - 1, greet, 0)
    pl.semaphore_wait(barrier, n - 1)

    def ask(i, carry):
        pltpu.make_async_remote_copy(
            src_ref=wanted.at[partner(i)], dst_ref=asked.at[me], send_sem=ask_send.at[i], recv_sem=ask_recv.at[me],
            device_id={"srv": partner(i)}, device_id_type=pl.DeviceIdType.MESH,
        ).start()
        return carry

    lax.fori_loop(0, n - 1, ask, 0)
    own = pltpu.make_async_copy(wanted.at[me], asked.at[me], own_sem)
    own.start()
    own.wait()
    near[blocks] = jnp.zeros((rows, width), near.dtype)
    far[blocks] = jnp.zeros((rows, width), far.dtype)

    def heard(i, carry):
        peer = partner(i)
        pltpu.make_async_copy(asked.at[peer], asked.at[peer], ask_recv.at[peer]).wait()
        pltpu.make_async_copy(wanted.at[peer], wanted.at[peer], ask_send.at[i]).wait()
        return carry

    lax.fori_loop(0, n - 1, heard, 0)
    local = pltpu.make_async_copy(asked, asked_now, own_sem)
    local.start()
    local.wait()
    cells = lax.broadcasted_iota(jnp.int32, (rows, width), 1)

    def chosen(peer, j):
        block = asked_now[peer, 0, j]
        return jnp.where(cells < tile_count[block], fields[block].astype(jnp.float32), 0.0).astype(fields.dtype)

    def send(i, carry):
        peer = partner(i)
        for j in range(capacity):
            outgoing[i, j] = chosen(peer, j)

        def start(target):
            pltpu.make_async_remote_copy(
                src_ref=outgoing.at[i], dst_ref=target.at[pl.ds(lax.rem(me, half) * capacity, capacity)],
                send_sem=send_sem.at[i], recv_sem=recv_sem.at[me],
                device_id={"srv": peer}, device_id_type=pl.DeviceIdType.MESH,
            ).start()

        @pl.when(peer // half == me // half)
        def _():
            start(near)

        @pl.when(peer // half != me // half)
        def _():
            start(far)

        return carry

    lax.fori_loop(0, n - 1, send, 0)
    for j in range(capacity):
        near[lax.rem(me, half) * capacity + j] = chosen(me, j)

    def arrive(target, i, first):
        piece = target.at[pl.ds(i * capacity, capacity)]
        pltpu.make_async_copy(piece, piece, recv_sem.at[first + i]).wait()

    def arrive_near(i, carry):
        @pl.when(i != lax.rem(me, half))
        def _():
            arrive(near, i, (me // half) * half)

        return carry

    lax.fori_loop(0, half, arrive_near, 0)
    load.wait()
    prefix[0] = jnp.zeros((rows, width), jnp.float32)

    def step(p, carry):
        part = contract(
            [near[near_src[p * UNIT + u]] for u in range(UNIT)], [held[near_slot[p * UNIT + u]] for u in range(UNIT)]
        )
        prefix[p + 1] = jnp.where(keep[p] == 1, prefix[p], 0.0) + part
        return carry

    lax.fori_loop(0, steps, step, 0)

    def pick(g, carry):
        totals[g] = jnp.where(used[g] == 1, prefix[last[g] + 1], 0.0)
        return carry

    lax.fori_loop(0, totals.shape[0], pick, 0)

    def finish(i, carry):
        pltpu.make_async_copy(outgoing.at[i], outgoing.at[i], send_sem.at[i]).wait()
        return carry

    def arrive_far(i, carry):
        arrive(far, i, (1 - me // half) * half)
        return carry

    lax.fori_loop(0, half, arrive_far, 0)
    lax.fori_loop(0, n - 1, finish, 0)


def exchange(n, n_rows, steps, tile_count, near_slot, near_src, keep, last, used, route, fields, weights):
    rows, width = fields.shape[1:]
    capacity = route.shape[1]
    blocks = n // 2 * capacity
    smem = pl.BlockSpec(memory_space=pltpu.SMEM)
    vmem = pl.BlockSpec(memory_space=pltpu.VMEM)
    hbm = pl.BlockSpec(memory_space=pl.ANY)
    wanted = jnp.broadcast_to(jnp.pad(route, ((0, 0), (0, 128 - capacity)))[:, None, :], (n, 8, 128))
    dma = pltpu.SemaphoreType.DMA
    return pl.pallas_call(
        functools.partial(exchange_kernel, n, steps),
        out_shape=[
            jax.ShapeDtypeStruct((blocks + 1, rows, width), fields.dtype),
            jax.ShapeDtypeStruct((blocks + 1, rows, width), fields.dtype),
            jax.ShapeDtypeStruct((n_rows, rows, width), jnp.float32),
        ],
        in_specs=[smem] * 6 + [vmem] * 2 + [hbm],
        out_specs=[vmem] * 3,
        scratch_shapes=[
            pltpu.VMEM((n, 8, 128), jnp.int32),
            pltpu.SMEM((n, 8, 128), jnp.int32),
            pltpu.VMEM((n - 1, capacity, rows, width), fields.dtype),
            pltpu.VMEM(weights.shape, weights.dtype),
            pltpu.VMEM((steps + 1, rows, width), jnp.float32),
            dma((n - 1,)),
            dma((n,)),
            dma((n - 1,)),
            dma((n,)),
            dma,
            dma,
        ],
        compiler_params=pltpu.CompilerParams(
            vmem_limit_bytes=LIMIT, collective_id=0, has_side_effects=True
        ),
    )(tile_count, near_slot, near_src, keep, last, used, wanted, fields, weights)


def product_kernel(first, last, n_rows, done, finish, starts, slot, src, near, far, w_hbm, prev, *refs):
    *outs, ring, acc, w_sem = refs
    zero = far.shape[0] - 1
    begin, end = starts[n_rows + first], starts[n_rows + last]

    def fetch(p, at):
        for u in range(UNIT):
            pltpu.make_async_copy(w_hbm.at[slot[p * UNIT + u]], ring.at[at, u], w_sem.at[at]).start()

    def step(x, p, at):
        pltpu.make_async_copy(ring.at[at], ring.at[at], w_sem.at[at]).wait()
        places = [src[p * UNIT + u] for u in range(UNIT)]
        acc[...] += contract([x[jnp.where(s < 0, zero, lax.rem(s, zero))] for s in places], [ring[at, u] for u in range(UNIT)])

    def left_over(p, carry):
        fetch(p, RING)
        step(near, p, RING)
        return carry

    def prime(p, carry):
        fetch(p, lax.rem(p, RING))
        return carry

    def far_step(p, carry):
        step(far, p, lax.rem(p, RING))

        @pl.when(p + RING < end)
        def _():
            fetch(p + RING, lax.rem(p, RING))

        return carry

    lax.fori_loop(begin, jnp.minimum(end, begin + RING), prime, 0)

    def bucket(g, carry):
        acc[...] = prev[g - first]
        lax.fori_loop(jnp.maximum(starts[g], done), starts[g + 1], left_over, 0)
        lax.fori_loop(starts[n_rows + g], starts[n_rows + g + 1], far_step, 0)
        finish(g - first, acc, outs)
        return carry

    lax.fori_loop(first, last, bucket, 0)


def products(starts, slot, src, near, far, w, prev, first, last, n_rows, done, finish, out_shape):
    rows, width = near.shape[1:]
    smem = pl.BlockSpec(memory_space=pltpu.SMEM)
    hbm = pl.BlockSpec(memory_space=pl.ANY)
    vmem = pl.BlockSpec(memory_space=pltpu.VMEM)
    n_slots = w.shape[0] * (last - first) // (2 * n_rows)
    return pl.pallas_call(
        functools.partial(product_kernel, first, last, n_rows, done, finish),
        out_shape=out_shape,
        in_specs=[smem] * 3 + [vmem] * 2 + [hbm, vmem],
        out_specs=jax.tree.map(lambda _: vmem, out_shape),
        scratch_shapes=[
            pltpu.VMEM((RING + 1, UNIT, width, width), w.dtype),
            pltpu.VMEM((rows, width), jnp.float32),
            pltpu.SemaphoreType.DMA((RING + 1,)),
        ],
        compiler_params=pltpu.CompilerParams(vmem_limit_bytes=LIMIT),
        cost_estimate=pl.CostEstimate(
            flops=4 * n_slots * rows * width * width, bytes_accessed=4 * n_slots * width * width, transcendentals=0
        ),
    )(starts, slot, src, near, far, w, prev)


def finish_rows(i, total, outs):
    out, head = outs

    @pl.when(i == 0)
    def _():
        head[...] = total[...]

    out[i] = total[...].astype(out.dtype)


def finish_excess(i, total, outs):
    outs[0][...] = total[...]


def shards(fields, tile_count, route, weights, block_src, destination_block, block_live):
    servers = lax.axis_size("srv")
    server = lax.axis_index("srv")
    held, rows, width = fields.shape
    slots = weights.shape[0]
    capacity = route.shape[2]
    band = DB_DEV
    n_rows = band + 1
    half = servers // 2
    blocks = half * capacity
    local = jnp.mod(destination_block - server * band, band * servers)
    entry, rank = block_src % capacity, block_src // capacity
    phase = (rank // half != server // half).astype(jnp.int32)
    source = phase * blocks + (rank % half) * capacity + entry
    steps_max = -(-slots // UNIT) + 2 * n_rows
    starts, slot, src = plan(phase * n_rows + local, block_live == 1, 2 * n_rows, source, steps_max)
    done = slots // UNIT // 2 + n_rows
    near_ends = jnp.minimum(starts[: n_rows + 1], done)
    lead = jnp.arange(done, dtype=jnp.int32)
    keep = 1 - jnp.max((lead[:, None] == starts[None, :n_rows]).astype(jnp.int32), axis=1)
    place = jnp.arange(done * UNIT, dtype=jnp.int32)
    inside = (place < near_ends[n_rows] * UNIT) & (src[: done * UNIT] >= 0)
    near_src = jnp.where(inside, src[: done * UNIT], blocks)
    used = (near_ends[1:] > near_ends[:-1]).astype(jnp.int32)
    last = jnp.maximum(near_ends[1:] - 1, 0)
    near, far, totals = exchange(
        servers, n_rows, done, tile_count, slot[: done * UNIT], near_src, keep, last, used, route[0], fields, weights
    )
    piece = jax.ShapeDtypeStruct((rows, width), jnp.float32)
    shared = (n_rows, done)
    (excess,) = products(
        starts, slot, src, near, far, weights, totals[band:], band, n_rows, *shared, finish_excess, (piece,)
    )
    arrived = lax.ppermute(excess, "srv", [(i, (i + 1) % servers) for i in range(servers)])
    body = jax.ShapeDtypeStruct((band, rows, width), jnp.bfloat16)
    out, head = products(
        starts, slot, src, near, far, weights, totals[:band], 0, band, *shared, finish_rows, (body, piece)
    )
    return out.at[0].set((head + arrived).astype(jnp.bfloat16))


def solution(mesh):
    in_specs = (
        P(("groups", "srv"), None, None),
        P("srv"),
        P("srv", None, None),
        P("srv", None, None),
        P("srv"),
        P("srv"),
        P("srv"),
    )
    out_specs = P(("groups", "srv"), None, None)
    return jax.shard_map(shards, mesh=mesh, in_specs=in_specs, out_specs=out_specs, check_vma=False)
```

```python
import functools

import jax
import jax.numpy as jnp
from jax import lax
from jax.experimental import pallas as pl
from jax.experimental.pallas import tpu as pltpu
from jax.sharding import PartitionSpec as P

DB_DEV = 16
UNIT = 4
LIMIT = 54 << 20


def plan(bucket, valid, n_buckets, source, steps_max):
    slots = bucket.shape[0]
    zero_source = -1
    ids = jnp.arange(n_buckets, dtype=jnp.int32)
    member = (bucket[None, :] == ids[:, None]) & valid[None, :]
    steps = (jnp.sum(member.astype(jnp.int32), axis=1) + UNIT - 1) // UNIT
    edges = jnp.arange(n_buckets + 1, dtype=jnp.int32)
    starts = jnp.sum(jnp.where(ids[None, :] < edges[:, None], steps[None, :], 0), axis=1)
    index = jnp.arange(slots, dtype=jnp.int32)
    before = jnp.sum(
        ((bucket[None, :] == bucket[:, None]) & valid[None, :] & (index[None, :] < index[:, None])).astype(jnp.int32),
        axis=1,
    )
    own = jnp.sum(jnp.where(ids[None, :] < bucket[:, None], steps[None, :], 0), axis=1)
    place = jnp.where(valid, own * UNIT + before, -1)
    places = jnp.arange(steps_max * UNIT, dtype=jnp.int32)
    hit = places[:, None] == place[None, :]
    slot = jnp.sum(jnp.where(hit, (index + jnp.where(before == 0, slots, 0))[None, :], 0), axis=1)
    src = jnp.sum(jnp.where(hit, source[None, :] - zero_source, 0), axis=1) + zero_source
    return starts, slot, src


def contract(blocks, factors):
    return lax.dot_general(
        jnp.concatenate(blocks, axis=1),
        jnp.concatenate(factors, axis=1),
        (((1,), (1,)), ((), ())),
        preferred_element_type=jnp.float32,
    )


def exchange_kernel(
    n, steps, tile_count, starts, slot, src,
    wanted, fields, w_hbm,
    near, far, totals, shared,
    asked, asked_now, outgoing, held, prefix,
    ask_send, ask_recv, send_sem, recv_sem, own_sem, w_sem,
):
    me = lax.axis_index("srv")
    half = n // 2
    rows, width = fields.shape[1:]
    capacity = outgoing.shape[1]
    blocks = half * capacity
    load = pltpu.make_async_copy(w_hbm, held, w_sem)
    load.start()

    def partner(i):
        return lax.rem(me + half + ((i + 1) // 2) * (2 * ((i + 1) % 2) - 1), n)

    barrier = pltpu.get_barrier_semaphore()

    def greet(i, carry):
        pl.semaphore_signal(barrier, inc=1, device_id={"srv": partner(i)}, device_id_type=pl.DeviceIdType.MESH)
        return carry

    lax.fori_loop(0, n - 1, greet, 0)
    pl.semaphore_wait(barrier, n - 1)

    def ask(i, carry):
        pltpu.make_async_remote_copy(
            src_ref=wanted.at[partner(i)], dst_ref=asked.at[me], send_sem=ask_send.at[i], recv_sem=ask_recv.at[me],
            device_id={"srv": partner(i)}, device_id_type=pl.DeviceIdType.MESH,
        ).start()
        return carry

    lax.fori_loop(0, n - 1, ask, 0)
    own = pltpu.make_async_copy(wanted.at[me], asked.at[me], own_sem)
    own.start()
    own.wait()
    near[blocks] = jnp.zeros((rows, width), near.dtype)
    far[blocks] = jnp.zeros((rows, width), far.dtype)

    def heard(i, carry):
        peer = partner(i)
        pltpu.make_async_copy(asked.at[peer], asked.at[peer], ask_recv.at[peer]).wait()
        pltpu.make_async_copy(wanted.at[peer], wanted.at[peer], ask_send.at[i]).wait()
        return carry

    lax.fori_loop(0, n - 1, heard, 0)
    local = pltpu.make_async_copy(asked, asked_now, own_sem)
    local.start()
    local.wait()
    cells = lax.broadcasted_iota(jnp.int32, (rows, width), 1)

    def chosen(peer, j):
        block = asked_now[peer, 0, j]
        return jnp.where(cells < tile_count[block], fields[block].astype(jnp.float32), 0.0).astype(fields.dtype)

    def send(i, carry):
        peer = partner(i)
        for j in range(capacity):
            outgoing[i, j] = chosen(peer, j)

        def start(target):
            pltpu.make_async_remote_copy(
                src_ref=outgoing.at[i], dst_ref=target.at[pl.ds(lax.rem(me, half) * capacity, capacity)],
                send_sem=send_sem.at[i], recv_sem=recv_sem.at[me],
                device_id={"srv": peer}, device_id_type=pl.DeviceIdType.MESH,
            ).start()

        @pl.when(peer // half == me // half)
        def _():
            start(near)

        @pl.when(peer // half != me // half)
        def _():
            start(far)

        return carry

    lax.fori_loop(0, n - 1, send, 0)
    for j in range(capacity):
        near[lax.rem(me, half) * capacity + j] = chosen(me, j)

    def arrive(target, i, first):
        piece = target.at[pl.ds(i * capacity, capacity)]
        pltpu.make_async_copy(piece, piece, recv_sem.at[first + i]).wait()

    def arrive_near(i, carry):
        @pl.when(i != lax.rem(me, half))
        def _():
            arrive(near, i, (me // half) * half)

        return carry

    lax.fori_loop(0, half, arrive_near, 0)
    load.wait()
    prefix[0] = jnp.zeros((rows, width), jnp.float32)
    slots, n_rows, last_step = w_hbm.shape[0], totals.shape[0] + 1, slot.shape[0] // UNIT - 1

    def run(x, phase):
        base, end = starts[phase * n_rows], starts[(phase + 1) * n_rows]

        def step(q, carry):
            real = base + q < end
            p = jnp.minimum(base + q, last_step) * UNIT
            places = [src[p + u] for u in range(UNIT)]
            places = [jnp.where(real & (s >= 0), s - phase * blocks, blocks) for s in places]
            part = contract([x[s] for s in places], [held[lax.rem(slot[p + u], slots)] for u in range(UNIT)])
            prefix[q + 1] = jnp.where(slot[p] < slots, prefix[q], 0.0) + part
            return carry

        lax.fori_loop(0, steps, step, 0)

    def sums(g, phase):
        base = starts[phase * n_rows]
        low = jnp.minimum(starts[phase * n_rows + g] - base, steps)
        high = jnp.minimum(starts[phase * n_rows + g + 1] - base, steps)
        return jnp.where(high > low, prefix[high], 0.0)

    run(near, 0)

    def pick(g, carry):
        totals[g] = sums(g, 0)
        return carry

    lax.fori_loop(0, n_rows - 1, pick, 0)
    shared[...] = sums(n_rows - 1, 0)

    def finish(i, carry):
        pltpu.make_async_copy(outgoing.at[i], outgoing.at[i], send_sem.at[i]).wait()
        return carry

    def arrive_far(i, carry):
        arrive(far, i, (1 - me // half) * half)
        return carry

    lax.fori_loop(0, half, arrive_far, 0)
    run(far, 1)

    def add(g, carry):
        totals[g] += sums(g, 1)
        return carry

    lax.fori_loop(0, n_rows - 1, add, 0)
    shared[...] += sums(n_rows - 1, 1)
    lax.fori_loop(0, n - 1, finish, 0)


def exchange(n, n_rows, steps, tile_count, starts, slot, src, route, fields, weights):
    rows, width = fields.shape[1:]
    capacity = route.shape[1]
    blocks = n // 2 * capacity
    smem = pl.BlockSpec(memory_space=pltpu.SMEM)
    vmem = pl.BlockSpec(memory_space=pltpu.VMEM)
    hbm = pl.BlockSpec(memory_space=pl.ANY)
    wanted = jnp.broadcast_to(jnp.pad(route, ((0, 0), (0, 128 - capacity)))[:, None, :], (n, 8, 128))
    dma = pltpu.SemaphoreType.DMA
    return pl.pallas_call(
        functools.partial(exchange_kernel, n, steps),
        out_shape=[
            jax.ShapeDtypeStruct((blocks + 1, rows, width), fields.dtype),
            jax.ShapeDtypeStruct((blocks + 1, rows, width), fields.dtype),
            jax.ShapeDtypeStruct((n_rows - 1, rows, width), jnp.float32),
            jax.ShapeDtypeStruct((rows, width), jnp.float32),
        ],
        in_specs=[smem] * 4 + [vmem] * 2 + [hbm],
        out_specs=[vmem] * 4,
        scratch_shapes=[
            pltpu.VMEM((n, 8, 128), jnp.int32),
            pltpu.SMEM((n, 8, 128), jnp.int32),
            pltpu.VMEM((n - 1, capacity, rows, width), fields.dtype),
            pltpu.VMEM(weights.shape, weights.dtype),
            pltpu.VMEM((steps + 1, rows, width), jnp.float32),
            dma((n - 1,)),
            dma((n,)),
            dma((n - 1,)),
            dma((n,)),
            dma,
            dma,
        ],
        compiler_params=pltpu.CompilerParams(
            vmem_limit_bytes=LIMIT, collective_id=0, has_side_effects=True
        ),
    )(tile_count, starts, slot, src, wanted, fields, weights)


def rest_kernel(first, last, n_rows, done, starts, slot, src, near, far, w_hbm, prev, *refs):
    *arrived, out, held, block, acc, w_sem, x_sem = refs
    zero = far.shape[0] - 1

    def left_over(x, p, carry):
        for u in range(UNIT):
            s = src[p * UNIT + u]
            factor = pltpu.make_async_copy(w_hbm.at[lax.rem(slot[p * UNIT + u], w_hbm.shape[0])], held, w_sem)
            factor.start()
            piece = pltpu.make_async_copy(x.at[jnp.where(s < 0, zero, lax.rem(s, zero))], block, x_sem)
            piece.start()
            factor.wait()
            piece.wait()
            acc[...] += contract([block[...]], [held[...]])
        return carry

    def bucket(g, carry):
        acc[...] = prev[g - first]
        lax.fori_loop(jnp.maximum(starts[g], done), starts[g + 1], functools.partial(left_over, near), 0)
        lax.fori_loop(
            jnp.maximum(starts[n_rows + g], starts[n_rows] + done), starts[n_rows + g + 1],
            functools.partial(left_over, far), 0,
        )
        if arrived:

            @pl.when(g == first)
            def _():
                acc[...] += arrived[0][...]

        out[g - first] = acc[...].astype(out.dtype)
        return carry

    lax.fori_loop(first, last, bucket, 0)


def rest(starts, slot, src, near, far, w, prev, first, last, n_rows, done, dtype, arrived=()):
    rows, width = near.shape[1:]
    smem = pl.BlockSpec(memory_space=pltpu.SMEM)
    hbm = pl.BlockSpec(memory_space=pl.ANY)
    vmem = pl.BlockSpec(memory_space=pltpu.VMEM)
    return pl.pallas_call(
        functools.partial(rest_kernel, first, last, n_rows, done),
        out_shape=jax.ShapeDtypeStruct((last - first, rows, width), dtype),
        in_specs=[smem] * 3 + [hbm] * 3 + [vmem] * (1 + len(arrived)),
        out_specs=vmem,
        scratch_shapes=[
            pltpu.VMEM((width, width), w.dtype),
            pltpu.VMEM((rows, width), near.dtype),
            pltpu.VMEM((rows, width), jnp.float32),
            pltpu.SemaphoreType.DMA,
            pltpu.SemaphoreType.DMA,
        ],
        compiler_params=pltpu.CompilerParams(vmem_limit_bytes=LIMIT),
    )(starts, slot, src, near, far, w, prev, *arrived)


def shards(fields, tile_count, route, weights, block_src, destination_block, block_live):
    servers = lax.axis_size("srv")
    server = lax.axis_index("srv")
    held, rows, width = fields.shape
    slots = weights.shape[0]
    capacity = route.shape[2]
    band = DB_DEV
    n_rows = band + 1
    half = servers // 2
    blocks = half * capacity
    local = jnp.mod(destination_block - server * band, band * servers)
    entry, rank = block_src % capacity, block_src // capacity
    phase = (rank // half != server // half).astype(jnp.int32)
    source = phase * blocks + (rank % half) * capacity + entry
    steps_max = -(-slots // UNIT) + 2 * n_rows
    starts, slot, src = plan(phase * n_rows + local, block_live == 1, 2 * n_rows, source, steps_max)
    done = slots // UNIT // 2 + n_rows
    near, far, totals, shared = exchange(
        servers, n_rows, done, tile_count, starts, slot, src, route[0], fields, weights
    )
    operands = (starts, slot, src, near, far, weights)
    excess = rest(*operands, shared[None], band, n_rows, n_rows, done, jnp.float32)[0]
    arrived = lax.ppermute(excess, "srv", [(i, (i + 1) % servers) for i in range(servers)])
    return rest(*operands, totals, 0, band, n_rows, done, jnp.bfloat16, (arrived,))


def solution(mesh):
    in_specs = (
        P(("groups", "srv"), None, None),
        P("srv"),
        P("srv", None, None),
        P("srv", None, None),
        P("srv"),
        P("srv"),
        P("srv"),
    )
    out_specs = P(("groups", "srv"), None, None)
    return jax.shard_map(shards, mesh=mesh, in_specs=in_specs, out_specs=out_specs, check_vma=False)
```

```python
import functools

import jax
import jax.numpy as jnp
from jax import lax
from jax.experimental import pallas as pl
from jax.experimental.pallas import tpu as pltpu
from jax.sharding import PartitionSpec as P

DB_DEV = 16
UNIT = 4
RING = 24
LIMIT = 54 << 20


def plan(bucket, valid, n_buckets, source, steps_max):
    slots = bucket.shape[0]
    zero_source = -1
    ids = jnp.arange(n_buckets, dtype=jnp.int32)
    member = (bucket[None, :] == ids[:, None]) & valid[None, :]
    steps = (jnp.sum(member.astype(jnp.int32), axis=1) + UNIT - 1) // UNIT
    edges = jnp.arange(n_buckets + 1, dtype=jnp.int32)
    starts = jnp.sum(jnp.where(ids[None, :] < edges[:, None], steps[None, :], 0), axis=1)
    index = jnp.arange(slots, dtype=jnp.int32)
    before = jnp.sum(
        ((bucket[None, :] == bucket[:, None]) & valid[None, :] & (index[None, :] < index[:, None])).astype(jnp.int32),
        axis=1,
    )
    own = jnp.sum(jnp.where(ids[None, :] < bucket[:, None], steps[None, :], 0), axis=1)
    place = jnp.where(valid, own * UNIT + before, -1)
    places = jnp.arange(steps_max * UNIT, dtype=jnp.int32)
    hit = places[:, None] == place[None, :]
    slot = jnp.sum(jnp.where(hit, (index + jnp.where(before == 0, slots, 0))[None, :], 0), axis=1)
    src = jnp.sum(jnp.where(hit, source[None, :] - zero_source, 0), axis=1) + zero_source
    return starts, slot, src


def contract(blocks, factors):
    return lax.dot_general(
        jnp.concatenate(blocks, axis=1),
        jnp.concatenate(factors, axis=1),
        (((1,), (1,)), ((), ())),
        preferred_element_type=jnp.float32,
    )


def exchange_kernel(
    n, steps, tile_count, starts, slot, src,
    wanted, fields, w_hbm,
    near, far, totals, shared,
    asked, asked_now, outgoing, held, prefix,
    ask_send, ask_recv, send_sem, recv_sem, own_sem, w_sem,
):
    me = lax.axis_index("srv")
    half = n // 2
    rows, width = fields.shape[1:]
    capacity = outgoing.shape[1]
    blocks = half * capacity
    load = pltpu.make_async_copy(w_hbm, held, w_sem)
    load.start()

    def partner(i):
        return lax.rem(me + half + ((i + 1) // 2) * (2 * ((i + 1) % 2) - 1), n)

    barrier = pltpu.get_barrier_semaphore()

    def greet(i, carry):
        pl.semaphore_signal(barrier, inc=1, device_id={"srv": partner(i)}, device_id_type=pl.DeviceIdType.MESH)
        return carry

    lax.fori_loop(0, n - 1, greet, 0)
    pl.semaphore_wait(barrier, n - 1)

    def ask(i, carry):
        pltpu.make_async_remote_copy(
            src_ref=wanted.at[partner(i)], dst_ref=asked.at[me], send_sem=ask_send.at[i], recv_sem=ask_recv.at[me],
            device_id={"srv": partner(i)}, device_id_type=pl.DeviceIdType.MESH,
        ).start()
        return carry

    lax.fori_loop(0, n - 1, ask, 0)
    own = pltpu.make_async_copy(wanted.at[me], asked.at[me], own_sem)
    own.start()
    own.wait()
    near[blocks] = jnp.zeros((rows, width), near.dtype)
    far[blocks] = jnp.zeros((rows, width), far.dtype)

    def heard(i, carry):
        peer = partner(i)
        pltpu.make_async_copy(asked.at[peer], asked.at[peer], ask_recv.at[peer]).wait()
        pltpu.make_async_copy(wanted.at[peer], wanted.at[peer], ask_send.at[i]).wait()
        return carry

    lax.fori_loop(0, n - 1, heard, 0)
    local = pltpu.make_async_copy(asked, asked_now, own_sem)
    local.start()
    local.wait()
    cells = lax.broadcasted_iota(jnp.int32, (rows, width), 1)

    def chosen(peer, j):
        block = asked_now[peer, 0, j]
        return jnp.where(cells < tile_count[block], fields[block].astype(jnp.float32), 0.0).astype(fields.dtype)

    def send(i, carry):
        peer = partner(i)
        for j in range(capacity):
            outgoing[i, j] = chosen(peer, j)

        def start(target):
            pltpu.make_async_remote_copy(
                src_ref=outgoing.at[i], dst_ref=target.at[pl.ds(lax.rem(me, half) * capacity, capacity)],
                send_sem=send_sem.at[i], recv_sem=recv_sem.at[me],
                device_id={"srv": peer}, device_id_type=pl.DeviceIdType.MESH,
            ).start()

        @pl.when(peer // half == me // half)
        def _():
            start(near)

        @pl.when(peer // half != me // half)
        def _():
            start(far)

        return carry

    lax.fori_loop(0, n - 1, send, 0)
    for j in range(capacity):
        near[lax.rem(me, half) * capacity + j] = chosen(me, j)

    def arrive(target, i, first):
        piece = target.at[pl.ds(i * capacity, capacity)]
        pltpu.make_async_copy(piece, piece, recv_sem.at[first + i]).wait()

    def arrive_near(i, carry):
        @pl.when(i != lax.rem(me, half))
        def _():
            arrive(near, i, (me // half) * half)

        return carry

    lax.fori_loop(0, half, arrive_near, 0)
    load.wait()
    prefix[0] = jnp.zeros((rows, width), jnp.float32)
    slots, n_rows, last_step = w_hbm.shape[0], totals.shape[0] + 1, slot.shape[0] // UNIT - 1

    def run(x, phase):
        base, end = starts[phase * n_rows], starts[(phase + 1) * n_rows]

        def step(q, carry):
            real = base + q < end
            p = jnp.minimum(base + q, last_step) * UNIT
            places = [src[p + u] for u in range(UNIT)]
            places = [jnp.where(real & (s >= 0), s - phase * blocks, blocks) for s in places]
            part = contract([x[s] for s in places], [held[lax.rem(slot[p + u], slots)] for u in range(UNIT)])
            prefix[q + 1] = jnp.where(slot[p] < slots, prefix[q], 0.0) + part
            return carry

        lax.fori_loop(0, steps, step, 0)

    def sums(g, phase):
        base = starts[phase * n_rows]
        low = jnp.minimum(starts[phase * n_rows + g] - base, steps)
        high = jnp.minimum(starts[phase * n_rows + g + 1] - base, steps)
        return jnp.where(high > low, prefix[high], 0.0)

    run(near, 0)

    def pick(g, carry):
        totals[g] = sums(g, 0)
        return carry

    lax.fori_loop(0, n_rows - 1, pick, 0)
    shared[...] = sums(n_rows - 1, 0)

    def finish(i, carry):
        pltpu.make_async_copy(outgoing.at[i], outgoing.at[i], send_sem.at[i]).wait()
        return carry

    def arrive_far(i, carry):
        arrive(far, i, (1 - me // half) * half)
        return carry

    lax.fori_loop(0, half, arrive_far, 0)
    lax.fori_loop(0, n - 1, finish, 0)


def exchange(n, n_rows, steps, tile_count, starts, slot, src, route, fields, weights):
    rows, width = fields.shape[1:]
    capacity = route.shape[1]
    blocks = n // 2 * capacity
    smem = pl.BlockSpec(memory_space=pltpu.SMEM)
    vmem = pl.BlockSpec(memory_space=pltpu.VMEM)
    hbm = pl.BlockSpec(memory_space=pl.ANY)
    wanted = jnp.broadcast_to(jnp.pad(route, ((0, 0), (0, 128 - capacity)))[:, None, :], (n, 8, 128))
    dma = pltpu.SemaphoreType.DMA
    return pl.pallas_call(
        functools.partial(exchange_kernel, n, steps),
        out_shape=[
            jax.ShapeDtypeStruct((blocks + 1, rows, width), fields.dtype),
            jax.ShapeDtypeStruct((blocks + 1, rows, width), fields.dtype),
            jax.ShapeDtypeStruct((n_rows - 1, rows, width), jnp.float32),
            jax.ShapeDtypeStruct((rows, width), jnp.float32),
        ],
        in_specs=[smem] * 4 + [vmem] * 2 + [hbm],
        out_specs=[vmem] * 4,
        scratch_shapes=[
            pltpu.VMEM((n, 8, 128), jnp.int32),
            pltpu.SMEM((n, 8, 128), jnp.int32),
            pltpu.VMEM((n - 1, capacity, rows, width), fields.dtype),
            pltpu.VMEM(weights.shape, weights.dtype),
            pltpu.VMEM((steps + 1, rows, width), jnp.float32),
            dma((n - 1,)),
            dma((n,)),
            dma((n - 1,)),
            dma((n,)),
            dma,
            dma,
        ],
        compiler_params=pltpu.CompilerParams(
            vmem_limit_bytes=LIMIT, collective_id=0, has_side_effects=True
        ),
    )(tile_count, starts, slot, src, wanted, fields, weights)


def product_kernel(first, last, n_rows, done, finish, starts, slot, src, near, far, w_hbm, prev, *refs):
    *outs, ring, acc, w_sem = refs
    zero = far.shape[0] - 1
    begin, end = starts[n_rows + first], starts[n_rows + last]

    def fetch(p, at):
        for u in range(UNIT):
            pltpu.make_async_copy(w_hbm.at[lax.rem(slot[p * UNIT + u], w_hbm.shape[0])], ring.at[at, u], w_sem.at[at]).start()

    def step(x, p, at):
        pltpu.make_async_copy(ring.at[at], ring.at[at], w_sem.at[at]).wait()
        places = [src[p * UNIT + u] for u in range(UNIT)]
        acc[...] += contract([x[jnp.where(s < 0, zero, lax.rem(s, zero))] for s in places], [ring[at, u] for u in range(UNIT)])

    def left_over(p, carry):
        fetch(p, RING)
        step(near, p, RING)
        return carry

    def prime(p, carry):
        fetch(p, lax.rem(p, RING))
        return carry

    def far_step(p, carry):
        step(far, p, lax.rem(p, RING))

        @pl.when(p + RING < end)
        def _():
            fetch(p + RING, lax.rem(p, RING))

        return carry

    lax.fori_loop(begin, jnp.minimum(end, begin + RING), prime, 0)

    def bucket(g, carry):
        acc[...] = prev[g - first]
        lax.fori_loop(jnp.maximum(starts[g], done), starts[g + 1], left_over, 0)
        lax.fori_loop(starts[n_rows + g], starts[n_rows + g + 1], far_step, 0)
        finish(g - first, acc, outs)
        return carry

    lax.fori_loop(first, last, bucket, 0)


def products(starts, slot, src, near, far, w, prev, first, last, n_rows, done, finish, out_shape):
    rows, width = near.shape[1:]
    smem = pl.BlockSpec(memory_space=pltpu.SMEM)
    hbm = pl.BlockSpec(memory_space=pl.ANY)
    vmem = pl.BlockSpec(memory_space=pltpu.VMEM)
    n_slots = w.shape[0] * (last - first) // (2 * n_rows)
    return pl.pallas_call(
        functools.partial(product_kernel, first, last, n_rows, done, finish),
        out_shape=out_shape,
        in_specs=[smem] * 3 + [vmem] * 2 + [hbm, vmem],
        out_specs=jax.tree.map(lambda _: vmem, out_shape),
        scratch_shapes=[
            pltpu.VMEM((RING + 1, UNIT, width, width), w.dtype),
            pltpu.VMEM((rows, width), jnp.float32),
            pltpu.SemaphoreType.DMA((RING + 1,)),
        ],
        compiler_params=pltpu.CompilerParams(vmem_limit_bytes=LIMIT),
        cost_estimate=pl.CostEstimate(
            flops=4 * n_slots * rows * width * width, bytes_accessed=4 * n_slots * width * width, transcendentals=0
        ),
    )(starts, slot, src, near, far, w, prev)


def finish_rows(i, total, outs):
    out, head = outs

    @pl.when(i == 0)
    def _():
        head[...] = total[...]

    out[i] = total[...].astype(out.dtype)


def finish_excess(i, total, outs):
    outs[0][...] = total[...]


def shards(fields, tile_count, route, weights, block_src, destination_block, block_live):
    servers = lax.axis_size("srv")
    server = lax.axis_index("srv")
    held, rows, width = fields.shape
    slots = weights.shape[0]
    capacity = route.shape[2]
    band = DB_DEV
    n_rows = band + 1
    half = servers // 2
    blocks = half * capacity
    local = jnp.mod(destination_block - server * band, band * servers)
    entry, rank = block_src % capacity, block_src // capacity
    phase = (rank // half != server // half).astype(jnp.int32)
    source = phase * blocks + (rank % half) * capacity + entry
    steps_max = -(-slots // UNIT) + 2 * n_rows
    starts, slot, src = plan(phase * n_rows + local, block_live == 1, 2 * n_rows, source, steps_max)
    done = slots // UNIT // 2 + n_rows
    near, far, totals, shared = exchange(
        servers, n_rows, done, tile_count, starts, slot, src, route[0], fields, weights
    )
    operands = (starts, slot, src, near, far, weights)
    piece = jax.ShapeDtypeStruct((rows, width), jnp.float32)
    common = (n_rows, done)
    (excess,) = products(*operands, shared[None], band, n_rows, *common, finish_excess, (piece,))
    arrived = lax.ppermute(excess, "srv", [(i, (i + 1) % servers) for i in range(servers)])
    body = jax.ShapeDtypeStruct((band, rows, width), jnp.bfloat16)
    out, head = products(*operands, totals, 0, band, *common, finish_rows, (body, piece))
    return out.at[0].set((head + arrived).astype(jnp.bfloat16))


def solution(mesh):
    in_specs = (
        P(("groups", "srv"), None, None),
        P("srv"),
        P("srv", None, None),
        P("srv", None, None),
        P("srv"),
        P("srv"),
        P("srv"),
    )
    out_specs = P(("groups", "srv"), None, None)
    return jax.shard_map(shards, mesh=mesh, in_specs=in_specs, out_specs=out_specs, check_vma=False)
```

```python
import functools

import jax
import jax.numpy as jnp
from jax import lax
from jax.experimental import pallas as pl
from jax.experimental.pallas import tpu as pltpu
from jax.sharding import PartitionSpec as P

DB_DEV = 16
UNIT = 8
RING = 12
LIMIT = 54 << 20


def plan(bucket, valid, n_buckets, source, steps_max):
    slots = bucket.shape[0]
    zero_source = -1
    ids = jnp.arange(n_buckets, dtype=jnp.int32)
    member = (bucket[None, :] == ids[:, None]) & valid[None, :]
    steps = (jnp.sum(member.astype(jnp.int32), axis=1) + UNIT - 1) // UNIT
    edges = jnp.arange(n_buckets + 1, dtype=jnp.int32)
    starts = jnp.sum(jnp.where(ids[None, :] < edges[:, None], steps[None, :], 0), axis=1)
    index = jnp.arange(slots, dtype=jnp.int32)
    before = jnp.sum(
        ((bucket[None, :] == bucket[:, None]) & valid[None, :] & (index[None, :] < index[:, None])).astype(jnp.int32),
        axis=1,
    )
    own = jnp.sum(jnp.where(ids[None, :] < bucket[:, None], steps[None, :], 0), axis=1)
    place = jnp.where(valid, own * UNIT + before, -1)
    places = jnp.arange(steps_max * UNIT, dtype=jnp.int32)
    hit = places[:, None] == place[None, :]
    slot = jnp.sum(jnp.where(hit, (index + jnp.where(before == 0, slots, 0))[None, :], 0), axis=1)
    src = jnp.sum(jnp.where(hit, source[None, :] - zero_source, 0), axis=1) + zero_source
    return starts, slot, src


def contract(blocks, factors):
    return lax.dot_general(
        jnp.concatenate(blocks, axis=1),
        jnp.concatenate(factors, axis=1),
        (((1,), (1,)), ((), ())),
        preferred_element_type=jnp.float32,
    )


def exchange_kernel(
    n, steps, tile_count, starts, slot, src,
    wanted, fields, w_hbm,
    near, far, totals, shared,
    asked, asked_now, outgoing, held, prefix,
    ask_send, ask_recv, send_sem, recv_sem, own_sem, w_sem,
):
    me = lax.axis_index("srv")
    half = n // 2
    rows, width = fields.shape[1:]
    capacity = outgoing.shape[1]
    blocks = half * capacity
    load = pltpu.make_async_copy(w_hbm, held, w_sem)
    load.start()

    def partner(i):
        return lax.rem(me + half + ((i + 1) // 2) * (2 * ((i + 1) % 2) - 1), n)

    barrier = pltpu.get_barrier_semaphore()

    def greet(i, carry):
        pl.semaphore_signal(barrier, inc=1, device_id={"srv": partner(i)}, device_id_type=pl.DeviceIdType.MESH)
        return carry

    lax.fori_loop(0, n - 1, greet, 0)
    pl.semaphore_wait(barrier, n - 1)

    def ask(i, carry):
        pltpu.make_async_remote_copy(
            src_ref=wanted.at[partner(i)], dst_ref=asked.at[me], send_sem=ask_send.at[i], recv_sem=ask_recv.at[me],
            device_id={"srv": partner(i)}, device_id_type=pl.DeviceIdType.MESH,
        ).start()
        return carry

    lax.fori_loop(0, n - 1, ask, 0)
    own = pltpu.make_async_copy(wanted.at[me], asked.at[me], own_sem)
    own.start()
    own.wait()
    near[blocks] = jnp.zeros((rows, width), near.dtype)
    far[blocks] = jnp.zeros((rows, width), far.dtype)

    def heard(i, carry):
        peer = partner(i)
        pltpu.make_async_copy(asked.at[peer], asked.at[peer], ask_recv.at[peer]).wait()
        pltpu.make_async_copy(wanted.at[peer], wanted.at[peer], ask_send.at[i]).wait()
        return carry

    lax.fori_loop(0, n - 1, heard, 0)
    local = pltpu.make_async_copy(asked, asked_now, own_sem)
    local.start()
    local.wait()
    cells = lax.broadcasted_iota(jnp.int32, (rows, width), 1)

    def chosen(peer, j):
        block = asked_now[peer, 0, j]
        return jnp.where(cells < tile_count[block], fields[block].astype(jnp.float32), 0.0).astype(fields.dtype)

    def send(i, carry):
        peer = partner(i)
        for j in range(capacity):
            outgoing[i, j] = chosen(peer, j)

        def start(target):
            pltpu.make_async_remote_copy(
                src_ref=outgoing.at[i], dst_ref=target.at[pl.ds(lax.rem(me, half) * capacity, capacity)],
                send_sem=send_sem.at[i], recv_sem=recv_sem.at[me],
                device_id={"srv": peer}, device_id_type=pl.DeviceIdType.MESH,
            ).start()

        @pl.when(peer // half == me // half)
        def _():
            start(near)

        @pl.when(peer // half != me // half)
        def _():
            start(far)

        return carry

    lax.fori_loop(0, n - 1, send, 0)
    for j in range(capacity):
        near[lax.rem(me, half) * capacity + j] = chosen(me, j)

    def arrive(target, i, first):
        piece = target.at[pl.ds(i * capacity, capacity)]
        pltpu.make_async_copy(piece, piece, recv_sem.at[first + i]).wait()

    def arrive_near(i, carry):
        @pl.when(i != lax.rem(me, half))
        def _():
            arrive(near, i, (me // half) * half)

        return carry

    lax.fori_loop(0, half, arrive_near, 0)
    load.wait()
    prefix[0] = jnp.zeros((rows, width), jnp.float32)
    slots, n_rows, last_step = w_hbm.shape[0], totals.shape[0] + 1, slot.shape[0] // UNIT - 1

    def run(x, phase):
        base, end = starts[phase * n_rows], starts[(phase + 1) * n_rows]

        def step(q, carry):
            real = base + q < end
            p = jnp.minimum(base + q, last_step) * UNIT
            places = [src[p + u] for u in range(UNIT)]
            places = [jnp.where(real & (s >= 0), s - phase * blocks, blocks) for s in places]
            part = contract([x[s] for s in places], [held[lax.rem(slot[p + u], slots)] for u in range(UNIT)])
            prefix[q + 1] = jnp.where(slot[p] < slots, prefix[q], 0.0) + part
            return carry

        lax.fori_loop(0, steps, step, 0)

    def sums(g, phase):
        base = starts[phase * n_rows]
        low = jnp.minimum(starts[phase * n_rows + g] - base, steps)
        high = jnp.minimum(starts[phase * n_rows + g + 1] - base, steps)
        return jnp.where(high > low, prefix[high], 0.0)

    run(near, 0)

    def pick(g, carry):
        totals[g] = sums(g, 0)
        return carry

    lax.fori_loop(0, n_rows - 1, pick, 0)
    shared[...] = sums(n_rows - 1, 0)

    def finish(i, carry):
        pltpu.make_async_copy(outgoing.at[i], outgoing.at[i], send_sem.at[i]).wait()
        return carry

    def arrive_far(i, carry):
        arrive(far, i, (1 - me // half) * half)
        return carry

    lax.fori_loop(0, half, arrive_far, 0)
    lax.fori_loop(0, n - 1, finish, 0)


def exchange(n, n_rows, steps, tile_count, starts, slot, src, route, fields, weights):
    rows, width = fields.shape[1:]
    capacity = route.shape[1]
    blocks = n // 2 * capacity
    smem = pl.BlockSpec(memory_space=pltpu.SMEM)
    vmem = pl.BlockSpec(memory_space=pltpu.VMEM)
    hbm = pl.BlockSpec(memory_space=pl.ANY)
    wanted = jnp.broadcast_to(jnp.pad(route, ((0, 0), (0, 128 - capacity)))[:, None, :], (n, 8, 128))
    dma = pltpu.SemaphoreType.DMA
    return pl.pallas_call(
        functools.partial(exchange_kernel, n, steps),
        out_shape=[
            jax.ShapeDtypeStruct((blocks + 1, rows, width), fields.dtype),
            jax.ShapeDtypeStruct((blocks + 1, rows, width), fields.dtype),
            jax.ShapeDtypeStruct((n_rows - 1, rows, width), jnp.float32),
            jax.ShapeDtypeStruct((rows, width), jnp.float32),
        ],
        in_specs=[smem] * 4 + [vmem] * 2 + [hbm],
        out_specs=[vmem] * 4,
        scratch_shapes=[
            pltpu.VMEM((n, 8, 128), jnp.int32),
            pltpu.SMEM((n, 8, 128), jnp.int32),
            pltpu.VMEM((n - 1, capacity, rows, width), fields.dtype),
            pltpu.VMEM(weights.shape, weights.dtype),
            pltpu.VMEM((steps + 1, rows, width), jnp.float32),
            dma((n - 1,)),
            dma((n,)),
            dma((n - 1,)),
            dma((n,)),
            dma,
            dma,
        ],
        compiler_params=pltpu.CompilerParams(
            vmem_limit_bytes=LIMIT, collective_id=0, has_side_effects=True
        ),
    )(tile_count, starts, slot, src, wanted, fields, weights)


def product_kernel(first, last, n_rows, done, finish, starts, slot, src, near, far, w_hbm, prev, *refs):
    *outs, ring, acc, w_sem = refs
    zero = far.shape[0] - 1
    begin, end = starts[n_rows + first], starts[n_rows + last]

    def fetch(p, at):
        for u in range(UNIT):
            pltpu.make_async_copy(w_hbm.at[lax.rem(slot[p * UNIT + u], w_hbm.shape[0])], ring.at[at, u], w_sem.at[at]).start()

    def step(x, p, at):
        pltpu.make_async_copy(ring.at[at], ring.at[at], w_sem.at[at]).wait()
        places = [src[p * UNIT + u] for u in range(UNIT)]
        acc[...] += contract([x[jnp.where(s < 0, zero, lax.rem(s, zero))] for s in places], [ring[at, u] for u in range(UNIT)])

    def left_over(p, carry):
        fetch(p, RING)
        step(near, p, RING)
        return carry

    def prime(p, carry):
        fetch(p, lax.rem(p, RING))
        return carry

    def far_step(p, carry):
        step(far, p, lax.rem(p, RING))

        @pl.when(p + RING < end)
        def _():
            fetch(p + RING, lax.rem(p, RING))

        return carry

    lax.fori_loop(begin, jnp.minimum(end, begin + RING), prime, 0)

    def bucket(g, carry):
        acc[...] = prev[g - first]
        lax.fori_loop(jnp.maximum(starts[g], done), starts[g + 1], left_over, 0)
        lax.fori_loop(starts[n_rows + g], starts[n_rows + g + 1], far_step, 0)
        finish(g - first, acc, outs)
        return carry

    lax.fori_loop(first, last, bucket, 0)


def products(starts, slot, src, near, far, w, prev, first, last, n_rows, done, finish, out_shape):
    rows, width = near.shape[1:]
    smem = pl.BlockSpec(memory_space=pltpu.SMEM)
    hbm = pl.BlockSpec(memory_space=pl.ANY)
    vmem = pl.BlockSpec(memory_space=pltpu.VMEM)
    n_slots = w.shape[0] * (last - first) // (2 * n_rows)
    return pl.pallas_call(
        functools.partial(product_kernel, first, last, n_rows, done, finish),
        out_shape=out_shape,
        in_specs=[smem] * 3 + [vmem] * 2 + [hbm, vmem],
        out_specs=jax.tree.map(lambda _: vmem, out_shape),
        scratch_shapes=[
            pltpu.VMEM((RING + 1, UNIT, width, width), w.dtype),
            pltpu.VMEM((rows, width), jnp.float32),
            pltpu.SemaphoreType.DMA((RING + 1,)),
        ],
        compiler_params=pltpu.CompilerParams(vmem_limit_bytes=LIMIT),
        cost_estimate=pl.CostEstimate(
            flops=4 * n_slots * rows * width * width, bytes_accessed=4 * n_slots * width * width, transcendentals=0
        ),
    )(starts, slot, src, near, far, w, prev)


def finish_rows(i, total, outs):
    out, head = outs

    @pl.when(i == 0)
    def _():
        head[...] = total[...]

    out[i] = total[...].astype(out.dtype)


def finish_excess(i, total, outs):
    outs[0][...] = total[...]


def shards(fields, tile_count, route, weights, block_src, destination_block, block_live):
    servers = lax.axis_size("srv")
    server = lax.axis_index("srv")
    held, rows, width = fields.shape
    slots = weights.shape[0]
    capacity = route.shape[2]
    band = DB_DEV
    n_rows = band + 1
    half = servers // 2
    blocks = half * capacity
    local = jnp.mod(destination_block - server * band, band * servers)
    entry, rank = block_src % capacity, block_src // capacity
    phase = (rank // half != server // half).astype(jnp.int32)
    source = phase * blocks + (rank % half) * capacity + entry
    steps_max = -(-slots // UNIT) + 2 * n_rows
    starts, slot, src = plan(phase * n_rows + local, block_live == 1, 2 * n_rows, source, steps_max)
    done = slots // UNIT // 2 + n_rows
    near, far, totals, shared = exchange(
        servers, n_rows, done, tile_count, starts, slot, src, route[0], fields, weights
    )
    operands = (starts, slot, src, near, far, weights)
    piece = jax.ShapeDtypeStruct((rows, width), jnp.float32)
    common = (n_rows, done)
    (excess,) = products(*operands, shared[None], band, n_rows, *common, finish_excess, (piece,))
    arrived = lax.ppermute(excess, "srv", [(i, (i + 1) % servers) for i in range(servers)])
    body = jax.ShapeDtypeStruct((band, rows, width), jnp.bfloat16)
    out, head = products(*operands, totals, 0, band, *common, finish_rows, (body, piece))
    return out.at[0].set((head + arrived).astype(jnp.bfloat16))


def solution(mesh):
    in_specs = (
        P(("groups", "srv"), None, None),
        P("srv"),
        P("srv", None, None),
        P("srv", None, None),
        P("srv"),
        P("srv"),
        P("srv"),
    )
    out_specs = P(("groups", "srv"), None, None)
    return jax.shard_map(shards, mesh=mesh, in_specs=in_specs, out_specs=out_specs, check_vma=False)
```

```python
import functools

import jax
import jax.numpy as jnp
from jax import lax
from jax.experimental import pallas as pl
from jax.experimental.pallas import tpu as pltpu
from jax.sharding import PartitionSpec as P

DB_DEV = 16
UNIT = 8
RING = 12
LIMIT = 54 << 20


def plan(bucket, valid, n_buckets, source, steps_max):
    slots = bucket.shape[0]
    zero_source = -1
    ids = jnp.arange(n_buckets, dtype=jnp.int32)
    member = (bucket[None, :] == ids[:, None]) & valid[None, :]
    steps = (jnp.sum(member.astype(jnp.int32), axis=1) + UNIT - 1) // UNIT
    edges = jnp.arange(n_buckets + 1, dtype=jnp.int32)
    starts = jnp.sum(jnp.where(ids[None, :] < edges[:, None], steps[None, :], 0), axis=1)
    index = jnp.arange(slots, dtype=jnp.int32)
    before = jnp.sum(
        ((bucket[None, :] == bucket[:, None]) & valid[None, :] & (index[None, :] < index[:, None])).astype(jnp.int32),
        axis=1,
    )
    own = jnp.sum(jnp.where(ids[None, :] < bucket[:, None], steps[None, :], 0), axis=1)
    place = jnp.where(valid, own * UNIT + before, -1)
    places = jnp.arange(steps_max * UNIT, dtype=jnp.int32)
    hit = places[:, None] == place[None, :]
    slot = jnp.sum(jnp.where(hit, (index + jnp.where(before == 0, slots, 0))[None, :], 0), axis=1)
    src = jnp.sum(jnp.where(hit, source[None, :] - zero_source, 0), axis=1) + zero_source
    return starts, slot, src


def contract(blocks, factors):
    return lax.dot_general(
        jnp.concatenate(blocks, axis=1),
        jnp.concatenate(factors, axis=1),
        (((1,), (1,)), ((), ())),
        preferred_element_type=jnp.float32,
    )


def exchange_kernel(
    n, steps, tile_count, starts, slot, src,
    wanted, fields, w_hbm,
    near, far, totals, shared,
    asked, asked_now, outgoing, held, prefix,
    ask_send, ask_recv, send_sem, recv_sem, own_sem, w_sem,
):
    me = lax.axis_index("srv")
    half = n // 2
    rows, width = fields.shape[1:]
    capacity = outgoing.shape[1]
    blocks = half * capacity
    load = pltpu.make_async_copy(w_hbm, held, w_sem)
    load.start()

    def partner(i):
        mine = (me // half) * half + lax.rem(me + i + 1, half)
        other = (1 - me // half) * half + lax.rem(me + i + 1, half)
        return jnp.where(i < half - 1, mine, other)

    barrier = pltpu.get_barrier_semaphore()

    def greet(i, carry):
        pl.semaphore_signal(barrier, inc=1, device_id={"srv": partner(i)}, device_id_type=pl.DeviceIdType.MESH)
        return carry

    lax.fori_loop(0, n - 1, greet, 0)
    pl.semaphore_wait(barrier, n - 1)

    def ask(i, carry):
        pltpu.make_async_remote_copy(
            src_ref=wanted.at[partner(i)], dst_ref=asked.at[me], send_sem=ask_send.at[i], recv_sem=ask_recv.at[me],
            device_id={"srv": partner(i)}, device_id_type=pl.DeviceIdType.MESH,
        ).start()
        return carry

    lax.fori_loop(0, n - 1, ask, 0)
    own = pltpu.make_async_copy(wanted.at[me], asked.at[me], own_sem)
    own.start()
    own.wait()
    near[blocks] = jnp.zeros((rows, width), near.dtype)
    far[blocks] = jnp.zeros((rows, width), far.dtype)

    def heard(i, carry):
        peer = partner(i)
        pltpu.make_async_copy(asked.at[peer], asked.at[peer], ask_recv.at[peer]).wait()
        pltpu.make_async_copy(wanted.at[peer], wanted.at[peer], ask_send.at[i]).wait()
        return carry

    lax.fori_loop(0, n - 1, heard, 0)
    local = pltpu.make_async_copy(asked, asked_now, own_sem)
    local.start()
    local.wait()
    cells = lax.broadcasted_iota(jnp.int32, (rows, width), 1)

    def chosen(peer, j):
        block = asked_now[peer, 0, j]
        return jnp.where(cells < tile_count[block], fields[block].astype(jnp.float32), 0.0).astype(fields.dtype)

    def send(i, carry):
        peer = partner(i)
        for j in range(capacity):
            outgoing[i, j] = chosen(peer, j)

        def start(target):
            pltpu.make_async_remote_copy(
                src_ref=outgoing.at[i], dst_ref=target.at[pl.ds(lax.rem(me, half) * capacity, capacity)],
                send_sem=send_sem.at[i], recv_sem=recv_sem.at[me],
                device_id={"srv": peer}, device_id_type=pl.DeviceIdType.MESH,
            ).start()

        @pl.when(peer // half == me // half)
        def _():
            start(near)

        @pl.when(peer // half != me // half)
        def _():
            start(far)

        return carry

    lax.fori_loop(0, n - 1, send, 0)
    for j in range(capacity):
        near[lax.rem(me, half) * capacity + j] = chosen(me, j)

    def arrive(target, i, first):
        piece = target.at[pl.ds(i * capacity, capacity)]
        pltpu.make_async_copy(piece, piece, recv_sem.at[first + i]).wait()

    def arrive_near(i, carry):
        @pl.when(i != lax.rem(me, half))
        def _():
            arrive(near, i, (me // half) * half)

        return carry

    lax.fori_loop(0, half, arrive_near, 0)
    load.wait()
    prefix[0] = jnp.zeros((rows, width), jnp.float32)
    slots, n_rows, last_step = w_hbm.shape[0], totals.shape[0] + 1, slot.shape[0] // UNIT - 1

    def run(x, phase):
        base, end = starts[phase * n_rows], starts[(phase + 1) * n_rows]

        def step(q, carry):
            real = base + q < end
            p = jnp.minimum(base + q, last_step) * UNIT
            places = [src[p + u] for u in range(UNIT)]
            places = [jnp.where(real & (s >= 0), s - phase * blocks, blocks) for s in places]
            part = contract([x[s] for s in places], [held[lax.rem(slot[p + u], slots)] for u in range(UNIT)])
            prefix[q + 1] = jnp.where(slot[p] < slots, prefix[q], 0.0) + part
            return carry

        lax.fori_loop(0, steps, step, 0)

    def sums(g, phase):
        base = starts[phase * n_rows]
        low = jnp.minimum(starts[phase * n_rows + g] - base, steps)
        high = jnp.minimum(starts[phase * n_rows + g + 1] - base, steps)
        return jnp.where(high > low, prefix[high], 0.0)

    run(near, 0)

    def pick(g, carry):
        totals[g] = sums(g, 0)
        return carry

    lax.fori_loop(0, n_rows - 1, pick, 0)
    shared[...] = sums(n_rows - 1, 0)

    def finish(i, carry):
        pltpu.make_async_copy(outgoing.at[i], outgoing.at[i], send_sem.at[i]).wait()
        return carry

    def arrive_far(i, carry):
        arrive(far, i, (1 - me // half) * half)
        return carry

    lax.fori_loop(0, half, arrive_far, 0)
    lax.fori_loop(0, n - 1, finish, 0)


def exchange(n, n_rows, steps, tile_count, starts, slot, src, route, fields, weights):
    rows, width = fields.shape[1:]
    capacity = route.shape[1]
    blocks = n // 2 * capacity
    smem = pl.BlockSpec(memory_space=pltpu.SMEM)
    vmem = pl.BlockSpec(memory_space=pltpu.VMEM)
    hbm = pl.BlockSpec(memory_space=pl.ANY)
    wanted = jnp.broadcast_to(jnp.pad(route, ((0, 0), (0, 128 - capacity)))[:, None, :], (n, 8, 128))
    dma = pltpu.SemaphoreType.DMA
    return pl.pallas_call(
        functools.partial(exchange_kernel, n, steps),
        out_shape=[
            jax.ShapeDtypeStruct((blocks + 1, rows, width), fields.dtype),
            jax.ShapeDtypeStruct((blocks + 1, rows, width), fields.dtype),
            jax.ShapeDtypeStruct((n_rows - 1, rows, width), jnp.float32),
            jax.ShapeDtypeStruct((rows, width), jnp.float32),
        ],
        in_specs=[smem] * 4 + [vmem] * 2 + [hbm],
        out_specs=[vmem] * 4,
        scratch_shapes=[
            pltpu.VMEM((n, 8, 128), jnp.int32),
            pltpu.SMEM((n, 8, 128), jnp.int32),
            pltpu.VMEM((n - 1, capacity, rows, width), fields.dtype),
            pltpu.VMEM(weights.shape, weights.dtype),
            pltpu.VMEM((steps + 1, rows, width), jnp.float32),
            dma((n - 1,)),
            dma((n,)),
            dma((n - 1,)),
            dma((n,)),
            dma,
            dma,
        ],
        compiler_params=pltpu.CompilerParams(
            vmem_limit_bytes=LIMIT, collective_id=0, has_side_effects=True
        ),
    )(tile_count, starts, slot, src, wanted, fields, weights)


def product_kernel(first, last, n_rows, done, finish, starts, slot, src, near, far, w_hbm, prev, *refs):
    *outs, ring, acc, w_sem = refs
    zero = far.shape[0] - 1
    begin, end = starts[n_rows + first], starts[n_rows + last]

    def fetch(p, at):
        for u in range(UNIT):
            pltpu.make_async_copy(w_hbm.at[lax.rem(slot[p * UNIT + u], w_hbm.shape[0])], ring.at[at, u], w_sem.at[at]).start()

    def step(x, p, at):
        pltpu.make_async_copy(ring.at[at], ring.at[at], w_sem.at[at]).wait()
        places = [src[p * UNIT + u] for u in range(UNIT)]
        acc[...] += contract([x[jnp.where(s < 0, zero, lax.rem(s, zero))] for s in places], [ring[at, u] for u in range(UNIT)])

    def left_over(p, carry):
        fetch(p, RING)
        step(near, p, RING)
        return carry

    def prime(p, carry):
        fetch(p, lax.rem(p, RING))
        return carry

    def far_step(p, carry):
        step(far, p, lax.rem(p, RING))

        @pl.when(p + RING < end)
        def _():
            fetch(p + RING, lax.rem(p, RING))

        return carry

    lax.fori_loop(begin, jnp.minimum(end, begin + RING), prime, 0)

    def bucket(g, carry):
        acc[...] = prev[g - first]
        lax.fori_loop(jnp.maximum(starts[g], done), starts[g + 1], left_over, 0)
        lax.fori_loop(starts[n_rows + g], starts[n_rows + g + 1], far_step, 0)
        finish(g - first, acc, outs)
        return carry

    lax.fori_loop(first, last, bucket, 0)


def products(starts, slot, src, near, far, w, prev, first, last, n_rows, done, finish, out_shape):
    rows, width = near.shape[1:]
    smem = pl.BlockSpec(memory_space=pltpu.SMEM)
    hbm = pl.BlockSpec(memory_space=pl.ANY)
    vmem = pl.BlockSpec(memory_space=pltpu.VMEM)
    n_slots = w.shape[0] * (last - first) // (2 * n_rows)
    return pl.pallas_call(
        functools.partial(product_kernel, first, last, n_rows, done, finish),
        out_shape=out_shape,
        in_specs=[smem] * 3 + [vmem] * 2 + [hbm, vmem],
        out_specs=jax.tree.map(lambda _: vmem, out_shape),
        scratch_shapes=[
            pltpu.VMEM((RING + 1, UNIT, width, width), w.dtype),
            pltpu.VMEM((rows, width), jnp.float32),
            pltpu.SemaphoreType.DMA((RING + 1,)),
        ],
        compiler_params=pltpu.CompilerParams(vmem_limit_bytes=LIMIT),
        cost_estimate=pl.CostEstimate(
            flops=4 * n_slots * rows * width * width, bytes_accessed=4 * n_slots * width * width, transcendentals=0
        ),
    )(starts, slot, src, near, far, w, prev)


def finish_rows(i, total, outs):
    out, head = outs

    @pl.when(i == 0)
    def _():
        head[...] = total[...]

    out[i] = total[...].astype(out.dtype)


def finish_excess(i, total, outs):
    outs[0][...] = total[...]


def shards(fields, tile_count, route, weights, block_src, destination_block, block_live):
    servers = lax.axis_size("srv")
    server = lax.axis_index("srv")
    held, rows, width = fields.shape
    slots = weights.shape[0]
    capacity = route.shape[2]
    band = DB_DEV
    n_rows = band + 1
    half = servers // 2
    blocks = half * capacity
    local = jnp.mod(destination_block - server * band, band * servers)
    entry, rank = block_src % capacity, block_src // capacity
    phase = (rank // half != server // half).astype(jnp.int32)
    source = phase * blocks + (rank % half) * capacity + entry
    steps_max = -(-slots // UNIT) + 2 * n_rows
    starts, slot, src = plan(phase * n_rows + local, block_live == 1, 2 * n_rows, source, steps_max)
    done = slots // UNIT // 2 + n_rows
    near, far, totals, shared = exchange(
        servers, n_rows, done, tile_count, starts, slot, src, route[0], fields, weights
    )
    operands = (starts, slot, src, near, far, weights)
    piece = jax.ShapeDtypeStruct((rows, width), jnp.float32)
    common = (n_rows, done)
    (excess,) = products(*operands, shared[None], band, n_rows, *common, finish_excess, (piece,))
    arrived = lax.ppermute(excess, "srv", [(i, (i + 1) % servers) for i in range(servers)])
    body = jax.ShapeDtypeStruct((band, rows, width), jnp.bfloat16)
    out, head = products(*operands, totals, 0, band, *common, finish_rows, (body, piece))
    return out.at[0].set((head + arrived).astype(jnp.bfloat16))


def solution(mesh):
    in_specs = (
        P(("groups", "srv"), None, None),
        P("srv"),
        P("srv", None, None),
        P("srv", None, None),
        P("srv"),
        P("srv"),
        P("srv"),
    )
    out_specs = P(("groups", "srv"), None, None)
    return jax.shard_map(shards, mesh=mesh, in_specs=in_specs, out_specs=out_specs, check_vma=False)
```
